32 devices in a mesh: sub: 8 (over z, y), mode: 4 (over x, core).
Axes of the slice: x: 2, y: 2, z: 4, core: 2. Of those that a mesh axis runs over, the one named last changes fastest.
Arguments:
- panels: bfloat16 [8, 2048, 768], P('sub', 'mode'), may hold values from -0.59765625 to 0.59765625
- eigvals: float32 [8, 2048], P('sub', 'mode'), may hold values from 0.5 to 20
- counts: int32 [8], P('sub'), may hold values from 512 to 2048, as said below
- separator_diag: float32 [8, 768], P('sub'), may hold values from 4 to 8
- separator_index_tables: int32 [8, 768], replicated, may hold values from 0 to 767, each once within a row
Outputs:
- condensed: float32 [768, 768], P('sub')
The draws below stay inside these ranges and needn't reach their ends.
Inputs may be any that keep to these rules, and one draw needn't show every extreme that they name: `counts`: every value from 512 to 2048 can occur, and both ends occur in every draw. `separator_index_tables`: each row is a permutation of 0 to 767.
All inputs are finite; a program needn't handle non-finite values.
Results may differ from the reference program's by a relative error of at most 0.0003.
Values sent between devices are 32-bit elements; how exact they have to be, the bound alone decides.
A program may use at most 64 MiB of HBM per device.

```python
import math
import jax
import jax.numpy as jnp
from jax import lax

SEP = 768
MODES = 2048
NSUB = 8


def draw_counts(key, part):
    key_base, key_high, key_low = jax.random.split(key, 3)
    values = jax.random.randint(key_base, (NSUB,), MODES // 4, MODES + 1, dtype=jnp.int32)
    high_pos = jax.random.randint(key_high, (), 0, NSUB, dtype=jnp.int32)
    low_pos = (high_pos + 1 + jax.random.randint(key_low, (), 0, NSUB - 1, dtype=jnp.int32)) % NSUB
    values = values.at[high_pos].set(MODES)
    values = values.at[low_pos].set(MODES // 4)
    return values


def block_scale(key, extent, pieces, least, high):
    def one(axis_at, shards_of):
        heights = jax.random.uniform(jax.random.fold_in(jax.random.fold_in(key, 6), axis_at), (shards_of,), jnp.float32, least / len(pieces), high / len(pieces))
        return jnp.repeat(jnp.exp(heights), extent[axis_at] // shards_of).reshape((-1,) + (1,) * (len(extent) - axis_at - 1))

    loudness = one(*pieces[0])
    for cut in pieces[1:]:
        loudness = loudness * one(*cut)
    return loudness


def bell_draw(key, dims, deviation, most, pieces=(), kind=jnp.bfloat16):
    level = block_scale(key, dims, pieces, -0.22, 0.18) if pieces else 1.0
    result = jax.random.normal(key, dims, jnp.float32) * deviation * level
    return jnp.minimum(jnp.maximum(result, -most), most).astype(kind)


def setup_inputs(seed: int = 0) -> dict:
    arg_keys = jax.random.split(jax.random.key(seed), 6)
    panels = bell_draw(arg_keys[0], (NSUB, MODES, SEP), 0.1, 0.59765625, ((0, 8), (1, 4)))
    eigvals = jnp.clip(jnp.exp(math.log(20.0) - 3.6888795 * jax.random.uniform(arg_keys[1], (NSUB, MODES), jnp.float32) ** block_scale(arg_keys[1], (NSUB, MODES), ((0, 8), (1, 4)), -0.2, 0.2)), 0.5, 20.0)
    counts = draw_counts(jax.random.fold_in(arg_keys[5], 71), 0)
    separator_diag = jnp.clip(4.0 + 4.0 * jax.random.uniform(arg_keys[3], (NSUB, SEP), jnp.float32) ** block_scale(arg_keys[3], (NSUB, SEP), ((0, 8),), -0.2, 0.2), 4.0, 8.0)
    separator_index_tables = jax.vmap(lambda own: jax.random.permutation(own, SEP))(jax.random.split(arg_keys[4], NSUB)).reshape((NSUB, SEP)).astype(jnp.int32)
    return dict(panels=panels, eigvals=eigvals, counts=counts, separator_diag=separator_diag, separator_index_tables=separator_index_tables)


def node_perm(separator_index_tables, level_number, nodes):
    span_rows = 2 ** level_number
    map_rows = nodes * span_rows + span_rows - 1
    shifted = (jnp.arange(SEP, dtype=jnp.int32) + 97 * level_number % SEP) % SEP
    return separator_index_tables[map_rows][:, shifted]

def relabel_equations(schur_remainder_patch, arrangement_list):
    rows_first = jnp.take(schur_remainder_patch, arrangement_list, axis=0)
    return jnp.take(rows_first.T, arrangement_list, axis=0).T

def leaf_tile(operands):
    panel_rows, eig_row, live_count, diag_row = operands
    live_mask = (jnp.arange(MODES, dtype=jnp.int32) < live_count).astype(jnp.float32)
    weighted = (panel_rows.astype(jnp.float32) * (live_mask / eig_row)[:, None]).astype(jnp.bfloat16)
    partial_sum = jnp.dot(weighted.T, panel_rows, preferred_element_type=jnp.float32)
    return jnp.diag(diag_row) - partial_sum

def reference(panels, eigvals, counts, separator_diag, separator_index_tables):
    piled_patches = lax.map(leaf_tile, (panels, eigvals, counts, separator_diag))
    levels_total = NSUB.bit_length() - 1
    for level_number in range(levels_total):
        count_now = piled_patches.shape[0]
        reorder_layers = node_perm(separator_index_tables, level_number, jnp.arange(count_now, dtype=jnp.int32))
        reordered_submatrix = jax.vmap(relabel_equations)(piled_patches, reorder_layers)
        piled_patches = reordered_submatrix[0::2] + reordered_submatrix[1::2]
    return piled_patches[0] * (1.0 / math.sqrt(NSUB))
```

```python
import functools
import math

import jax
import jax.numpy as jnp
from jax import lax
from jax.experimental import pallas as pl
from jax.experimental.pallas import tpu as pltpu
from jax.sharding import PartitionSpec as P

MESH = pl.DeviceIdType.MESH
NT = (((1,), (1,)), ((), ()))
LANES = 128


def plan(subs, modes):
    if subs == 8 and modes == 4:
        x, y, near, far = ("mode", 1), ("sub", 0), ("sub", 1), ("sub", 2)
        return [
            [(True, *x), (True, *y), (True, *near), (True, *far)],
            [(True, *y), (True, *near), (True, *far), (False, *x)],
            [(True, *near), (True, *x), (True, *y), (True, *far)],
        ], 2
    sub_bits, mode_bits = subs.bit_length() - 1, modes.bit_length() - 1
    steps = [(True, "sub", b) for b in range(sub_bits)]
    steps += [(False, "mode", b) for b in range(1, mode_bits)]
    return [steps] * 3, 1


def bit_of(value, bit):
    return (value // 2**bit) % 2


def body(subs, modes, parts, pieces, *refs):
    panels_ref, eig_ref, counts_ref, diag_ref, tables_ref, out_ref = refs[:6]
    wt, pt, to_core, from_core, fin, core_sems, fin_sems, cross_sems, send_sems, recv_sems = refs[6:16]
    steps = len(parts[0])
    accs = refs[16 : 16 + steps + 1]
    lands = refs[16 + steps + 1 :]
    count = len(parts)
    sub_me, mode_me = lax.axis_index("sub"), lax.axis_index("mode")
    core_me = mode_me % 2
    sep = panels_ref.shape[1]
    depth = panels_ref.shape[0]
    rows = sep // subs // pieces
    place = {"sub": sub_me, "mode": mode_me}

    def partner(axis, bit):
        here = place[axis]
        other = here + 2**bit * (1 - 2 * bit_of(here, bit))
        return (other, mode_me) if axis == "sub" else (sub_me, other)

    sibling = partner("mode", 0)
    links = sorted({step[1:] for part in parts for step in part} | {("mode", 0)})
    barrier = pltpu.get_barrier_semaphore()
    for axis, bit in links:
        pl.semaphore_signal(barrier, inc=1, device_id=partner(axis, bit), device_id_type=MESH)

    lanes = lax.broadcasted_iota(jnp.int32, (sep, sep), 1).astype(jnp.float32)
    first = lax.broadcasted_iota(jnp.int32, (sep, 1), 0).astype(jnp.float32)
    high_row = lax.broadcasted_iota(jnp.int32, (16, sep), 0) == 0

    def one_hot(index):
        return jnp.where(index == lanes, 1.0, 0.0).astype(jnp.bfloat16)

    index = first
    for level in reversed(range(subs.bit_length() - 1)):
        shifted = index + float(97 * level % sep)
        shifted = jnp.where(shifted >= sep, shifted - sep, shifted)
        row = tables_ref[pl.ds((sub_me // 2**level) * 2**level + 2**level - 1, 1), :]
        digits = jnp.where(high_row, row // 16, row % 16).astype(jnp.float32).astype(jnp.bfloat16)
        found = lax.dot_general(one_hot(shifted), digits, NT, preferred_element_type=jnp.float32)
        index = found[:, 0:1] * 16.0 + found[:, 1:2]
    moved = one_hot(index)

    live = lax.broadcasted_iota(jnp.int32, (1, depth), 1) + mode_me * depth < counts_ref[0]
    scale = jnp.where(live, 1.0, 0.0) / eig_ref[...]
    panels_t = lax.dot_general(moved, panels_ref[...], NT, preferred_element_type=jnp.float32)
    pt[...] = panels_t.astype(jnp.bfloat16)
    wt[...] = (panels_t * scale).astype(jnp.bfloat16)

    diag = diag_ref[...] * jnp.where(mode_me == 0, 1.0, 0.0)
    top = diag.astype(jnp.bfloat16).astype(jnp.float32)
    middle = (diag - top).astype(jnp.bfloat16).astype(jnp.float32)
    low = diag - top - middle
    pick = lax.broadcasted_iota(jnp.int32, (16, sep), 0)
    split = jnp.where(pick == 0, top, jnp.where(pick == 1, middle, jnp.where(pick == 2, low, 0.0)))
    got = lax.dot_general(moved, split.astype(jnp.bfloat16), NT, preferred_element_type=jnp.float32)
    diag_moved = got[:, 0:1] + got[:, 1:2] + got[:, 2:3]
    columns = lax.broadcasted_iota(jnp.int32, (sep, LANES), 1).astype(jnp.float32)

    def tile(core, p):
        start = pl.multiple_of((core * count + p) * LANES, LANES)
        product = lax.dot_general(
            wt[...], pt[pl.ds(start, LANES), :], NT, preferred_element_type=jnp.float32
        )
        on_diag = columns + start.astype(jnp.float32) == first
        return jnp.where(on_diag, diag_moved, 0.0) - product

    def slot_of(p, block):
        slot, taken = 0, 0
        for halve, axis, bit in parts[p]:
            if halve:
                if axis == "sub":
                    far = (bit_of(block // pieces, bit) + bit_of(sub_me, bit)) % 2
                else:
                    far = (bit_of(block % pieces, bit - 1) + bit_of(mode_me, bit)) % 2
                    taken = 1
                slot = slot * 2 + far
        return slot if taken else slot * pieces + block % pieces

    def core_copy(p):
        return pltpu.make_async_remote_copy(
            to_core.at[p], from_core.at[p], core_sems.at[0, p], core_sems.at[1, p], sibling, MESH
        )

    blocks = subs * pieces
    for p in range(count):
        value = tile(1 - core_me, p)
        for b in range(blocks):
            to_core[p, slot_of(p, b), :, :] = value[b * rows : (b + 1) * rows]
        if p == 0:
            pl.semaphore_wait(barrier, len(links))
        core_copy(p).start()

    sizes = []
    for p in range(count):
        n, own = blocks, []
        for halve, _, _ in parts[p]:
            n = n // 2 if halve else n
            own.append(n)
        sizes.append(own)

    def exchange(p, k):
        halve, axis, bit = parts[p][k]
        n = sizes[p][k]
        return pltpu.make_async_remote_copy(
            accs[k].at[p, pl.ds(n if halve else 0, n)],
            lands[k].at[p, pl.ds(0, n)],
            send_sems.at[p, k],
            recv_sems.at[p, k],
            partner(axis, bit),
            MESH,
        )

    for p in range(count):
        value = tile(core_me, p)
        for b in range(blocks):
            accs[0][p, slot_of(p, b), :, :] = value[b * rows : (b + 1) * rows]
    for p in range(count):
        core_copy(p).wait_recv()
        accs[0][p] = accs[0][p] + from_core[p]
        exchange(p, 0).start()

    cut = [any(halve and axis == "mode" for halve, axis, _ in part) for part in parts]
    piece_me = bit_of(mode_me, 1)

    def cross_copy(p):
        spot = fin.at[core_me, p, pl.ds(piece_me, 1)]
        return pltpu.make_async_remote_copy(
            spot, spot, cross_sems.at[0, p], cross_sems.at[1, p], partner("mode", 1), MESH
        )

    def final_copy(p):
        spot = fin.at[core_me, p]
        return pltpu.make_async_remote_copy(
            spot, spot, fin_sems.at[0, p], fin_sems.at[1, p], sibling, MESH
        )

    for k in range(steps):
        for p in range(count):
            n = sizes[p][k]
            exchange(p, k).wait_recv()
            total = accs[k][p, 0:n] + lands[k][p, 0:n]
            if k < steps - 1:
                accs[k + 1][p, 0:n] = total
                exchange(p, k + 1).start()
            elif cut[p]:
                fin[core_me, p, pl.ds(piece_me, 1)] = total
                cross_copy(p).start()
            else:
                fin[core_me, p] = total
                final_copy(p).start()
    for p in range(count):
        if cut[p]:
            cross_copy(p).wait_recv()
            final_copy(p).start()
    for p in range(count):
        final_copy(p).wait_recv()
    for c in range(2):
        for p in range(count):
            at = (c * count + p) * LANES
            for piece in range(pieces):
                out_ref[piece * rows : (piece + 1) * rows, at : at + LANES] = fin[c, p, piece]
    for p in range(count):
        core_copy(p).wait_send()
        for k in range(steps):
            exchange(p, k).wait_send()
        if cut[p]:
            cross_copy(p).wait_send()
        final_copy(p).wait_send()


def solution(mesh):
    subs, modes = mesh.shape["sub"], mesh.shape["mode"]
    parts, pieces = plan(subs, modes)

    def local(panels, eigvals, counts, separator_diag, tables):
        sep, depth = panels.shape[2], panels.shape[1]
        own = sep // subs
        rows = own // pieces
        count, steps, blocks = len(parts), len(parts[0]), subs * pieces
        f32 = jnp.float32

        def room(k):
            most = 0
            for part in parts:
                n = blocks
                for halve, _, _ in part[:k]:
                    n = n // 2 if halve else n
                most = max(most, n)
            return pltpu.VMEM((count, most, rows, LANES), f32)

        dma = pltpu.SemaphoreType.DMA
        root = pl.pallas_call(
            functools.partial(body, subs, modes, parts, pieces),
            out_shape=jax.ShapeDtypeStruct((own, sep), f32),
            in_specs=[
                pl.BlockSpec(memory_space=pltpu.VMEM),
                pl.BlockSpec(memory_space=pltpu.VMEM),
                pl.BlockSpec(memory_space=pltpu.SMEM),
                pl.BlockSpec(memory_space=pltpu.VMEM),
                pl.BlockSpec(memory_space=pltpu.VMEM),
            ],
            out_specs=pl.BlockSpec(memory_space=pltpu.VMEM),
            scratch_shapes=[
                pltpu.VMEM((sep, depth), jnp.bfloat16),
                pltpu.VMEM((sep, depth), jnp.bfloat16),
                pltpu.VMEM((count, blocks, rows, LANES), f32),
                pltpu.VMEM((count, blocks, rows, LANES), f32),
                pltpu.VMEM((2, count, pieces, rows, LANES), f32),
                dma((2, count)),
                dma((2, count)),
                dma((2, count)),
                dma((count, steps)),
                dma((count, steps)),
                *[room(k) for k in range(steps + 1)],
                *[room(k + 1) for k in range(steps)],
            ],
            compiler_params=pltpu.CompilerParams(
                collective_id=0, has_side_effects=True, vmem_limit_bytes=48 * 2**20
            ),
        )(panels[0], eigvals, counts, separator_diag, tables)
        return root * (1.0 / math.sqrt(subs))

    return jax.shard_map(
        local,
        mesh=mesh,
        in_specs=(P("sub", "mode", None), P("sub", "mode"), P("sub"), P("sub", None), P()),
        out_specs=P("sub", None),
        check_vma=False,
    )
```

```python
import functools
import math

import jax
import jax.numpy as jnp
from jax import lax
from jax.experimental import pallas as pl
from jax.experimental.pallas import tpu as pltpu
from jax.sharding import PartitionSpec as P

MESH = pl.DeviceIdType.MESH
NT = (((1,), (1,)), ((), ()))
LANES = 128


def plan(subs, modes):
    if subs == 8 and modes == 4:
        x, y, near, far = ("mode", 1), ("sub", 0), ("sub", 1), ("sub", 2)
        return [
            [(True, *x), (True, *y), (True, *near), (True, *far)],
            [(True, *y), (True, *near), (True, *far), (False, *x)],
            [(True, *near), (True, *x), (True, *y), (True, *far)],
        ], 2, 2
    sub_bits, mode_bits = subs.bit_length() - 1, modes.bit_length() - 1
    steps = [(True, "sub", b) for b in range(sub_bits)]
    steps += [(False, "mode", b) for b in range(1, mode_bits)]
    return [steps] * 3, 1, 1


def bit_of(value, bit):
    return (value // 2**bit) % 2


def body(subs, modes, column_parts, pieces, shares, *refs):
    panels_hbm, eig_hbm, counts_ref, diag_hbm, tables_hbm, out_ref = refs[:6]
    panels_ref, eig_ref, diag_ref, tables_ref, load_sems = refs[-5:]
    wt, pt, to_core, from_core, fin, core_sems, fin_sems, send_sems, recv_sems = refs[6:15]
    parts = [part for part in column_parts for _ in range(shares)]
    order = [q * shares + h for h in range(shares) for q in range(len(column_parts))]
    steps = len(parts[0])
    accs = refs[15 : 15 + steps + 1]
    lands = refs[15 + steps + 1 : -5]
    count, chunks = len(parts), len(column_parts)
    loads = [
        pltpu.make_async_copy(source, kept, load_sems.at[i])
        for i, (source, kept) in enumerate(
            [
                (tables_hbm, tables_ref),
                (panels_hbm, panels_ref),
                (eig_hbm, eig_ref),
                (diag_hbm, diag_ref),
            ]
        )
    ]
    for load in loads:
        load.start()
    sub_me, mode_me = lax.axis_index("sub"), lax.axis_index("mode")
    core_me = mode_me % 2
    sep = panels_ref.shape[1]
    depth = panels_ref.shape[0]
    rows = sep // subs // pieces // shares
    place = {"sub": sub_me, "mode": mode_me}

    def partner(axis, bit):
        here = place[axis]
        other = here + 2**bit * (1 - 2 * bit_of(here, bit))
        return (other, mode_me) if axis == "sub" else (sub_me, other)

    sibling = partner("mode", 0)
    links = sorted({step[1:] for part in parts for step in part} | {("mode", 0)})
    barrier = pltpu.get_barrier_semaphore()
    for axis, bit in links:
        pl.semaphore_signal(barrier, inc=1, device_id=partner(axis, bit), device_id_type=MESH)

    first = lax.broadcasted_iota(jnp.int32, (sep, 1), 0)
    across = (sub_me, partner("mode", 1)[1] + 1 - 2 * core_me) if pieces == 2 else None
    greeted = len(links) + (pieces == 2)
    if pieces == 2:
        pl.semaphore_signal(barrier, inc=1, device_id=across, device_id_type=MESH)

    runs = sep // LANES
    place_in_run = lax.broadcasted_iota(jnp.int32, (LANES, sep), 0)
    run_row = lax.broadcasted_iota(jnp.int32, (8, sep), 0)
    run_of = lax.broadcasted_iota(jnp.int32, (8, LANES), 0)
    loads[0].wait()
    index = lax.broadcasted_iota(jnp.int32, (1, sep), 1)
    for level in reversed(range(subs.bit_length() - 1)):
        index = index + 97 * level % sep
        index = jnp.where(index >= sep, index - sep, index)
        line = (sub_me // 2**level) * 2**level + 2**level - 1
        row = tables_ref[pl.ds(line, 1), :]
        table = jnp.zeros((8, LANES), jnp.int32)
        for run in range(runs):
            table = jnp.where(run_of == run, row[:, run * LANES : (run + 1) * LANES], table)
        digits = jnp.concatenate([table // 16, table % 16], axis=0).astype(jnp.float32).astype(jnp.bfloat16)
        mark = jnp.where(place_in_run == index % LANES, 1.0, 0.0).astype(jnp.bfloat16)
        found = jnp.dot(digits, mark, preferred_element_type=jnp.float32)
        value = jnp.where(run_row == index // LANES, found[0:8] * 16.0 + found[8:16], 0.0)
        index = jnp.sum(value, axis=0, keepdims=True).astype(jnp.int32)
    target = jnp.broadcast_to(index, (8, sep)).T[:, 0:1]
    lanes = lax.broadcasted_iota(jnp.int32, (sep, sep), 1)
    moved = jnp.where(target == lanes, 1.0, 0.0).astype(jnp.bfloat16)

    for load in loads[1:]:
        load.wait()
    live = lax.broadcasted_iota(jnp.int32, (1, depth), 1) + mode_me * depth < counts_ref[0]
    scale = jnp.where(live, 1.0, 0.0) / eig_ref[...]
    panels_t = lax.dot_general(moved, panels_ref[...], NT, preferred_element_type=jnp.float32)
    pt[...] = panels_t.astype(jnp.bfloat16)
    wt[...] = (panels_t * scale).astype(jnp.bfloat16)

    diag = diag_ref[...] * jnp.where(mode_me == 0, 1.0, 0.0)
    top = diag.astype(jnp.bfloat16).astype(jnp.float32)
    middle = (diag - top).astype(jnp.bfloat16).astype(jnp.float32)
    low = diag - top - middle
    pick = lax.broadcasted_iota(jnp.int32, (16, sep), 0)
    split = jnp.where(pick == 0, top, jnp.where(pick == 1, middle, jnp.where(pick == 2, low, 0.0)))
    got = lax.dot_general(moved, split.astype(jnp.bfloat16), NT, preferred_element_type=jnp.float32)
    diag_moved = got[:, 0:1] + got[:, 1:2] + got[:, 2:3]
    columns = lax.broadcasted_iota(jnp.int32, (sep, LANES), 1)

    def tile(core, p):
        start = pl.multiple_of((core * chunks + p) * LANES, LANES)
        product = lax.dot_general(
            wt[...], pt[pl.ds(start, LANES), :], NT, preferred_element_type=jnp.float32
        )
        on_diag = columns + start == first
        return jnp.where(on_diag, diag_moved, 0.0) - product

    def slot_of(p, block):
        slot, taken = 0, 0
        for halve, axis, bit in parts[p]:
            if halve:
                if axis == "sub":
                    far = (bit_of(block // pieces, bit) + bit_of(sub_me, bit)) % 2
                else:
                    far = (bit_of(block % pieces, bit - 1) + bit_of(mode_me, bit)) % 2
                    taken = 1
                slot = slot * 2 + far
        return slot if taken else slot * pieces + block % pieces

    def core_copy(p):
        return pltpu.make_async_remote_copy(
            to_core.at[p], from_core.at[p], core_sems.at[0, p], core_sems.at[1, p], sibling, MESH
        )

    blocks = subs * pieces
    def store_tile(kept, core, chunk):
        value = tile(core, chunk)
        for b in range(blocks):
            slot = slot_of(chunk * shares, b)
            for h in range(shares):
                at = (b * shares + h) * rows
                kept[chunk * shares + h, slot, :, :] = value[at : at + rows]

    for chunk in range(chunks):
        store_tile(to_core, 1 - core_me, chunk)
        if chunk == 0:
            pl.semaphore_wait(barrier, greeted)
        for h in range(shares):
            core_copy(chunk * shares + h).start()

    sizes = []
    for p in range(count):
        n, own = blocks, []
        for halve, _, _ in parts[p]:
            n = n // 2 if halve else n
            own.append(n)
        sizes.append(own)

    def exchange(p, k):
        halve, axis, bit = parts[p][k]
        n = sizes[p][k]
        return pltpu.make_async_remote_copy(
            accs[k].at[p, pl.ds(n if halve else 0, n)],
            lands[k].at[p, pl.ds(0, n)],
            send_sems.at[p, k],
            recv_sems.at[p, k],
            partner(axis, bit),
            MESH,
        )

    for chunk in range(chunks):
        store_tile(accs[0], core_me, chunk)
    for p in order:
        core_copy(p).wait_recv()
        accs[0][p] = accs[0][p] + from_core[p]
        exchange(p, 0).start()

    cut = [any(halve and axis == "mode" for halve, axis, _ in part) for part in parts]
    piece_me = bit_of(mode_me, 1)

    def last_copies(p):
        spot = fin.at[core_me, p, pl.ds(piece_me, 1)] if cut[p] else fin.at[core_me, p]
        targets = [sibling, partner("mode", 1), across] if cut[p] else [sibling]
        return [
            pltpu.make_async_remote_copy(spot, spot, fin_sems.at[0, p, i], fin_sems.at[1, p, i], target, MESH)
            for i, target in enumerate(targets)
        ]

    for k in range(steps):
        for p in order:
            n = sizes[p][k]
            exchange(p, k).wait_recv()
            total = accs[k][p, 0:n] + lands[k][p, 0:n]
            if k < steps - 1:
                accs[k + 1][p, 0:n] = total
                exchange(p, k + 1).start()
                continue
            if cut[p]:
                fin[core_me, p, pl.ds(piece_me, 1)] = total
            else:
                fin[core_me, p] = total
            for copy in last_copies(p):
                copy.start()
    for p in order:
        for copy in last_copies(p):
            copy.wait_recv()
    for c in range(2):
        for p in range(count):
            at = (c * chunks + p // shares) * LANES
            for piece in range(pieces):
                down = (piece * shares + p % shares) * rows
                out_ref[down : down + rows, at : at + LANES] = fin[c, p, piece]
    for p in range(count):
        core_copy(p).wait_send()
        for k in range(steps):
            exchange(p, k).wait_send()
        for copy in last_copies(p):
            copy.wait_send()


def solution(mesh):
    subs, modes = mesh.shape["sub"], mesh.shape["mode"]
    column_parts, pieces, shares = plan(subs, modes)
    parts = [part for part in column_parts for _ in range(shares)]

    def local(panels, eigvals, counts, separator_diag, tables):
        sep, depth = panels.shape[2], panels.shape[1]
        own = sep // subs
        rows = own // pieces // shares
        count, steps, blocks = len(parts), len(parts[0]), subs * pieces
        f32 = jnp.float32

        def room(k):
            most = 0
            for part in parts:
                n = blocks
                for halve, _, _ in part[:k]:
                    n = n // 2 if halve else n
                most = max(most, n)
            return pltpu.VMEM((count, most, rows, LANES), f32)

        dma = pltpu.SemaphoreType.DMA
        root = pl.pallas_call(
            functools.partial(body, subs, modes, column_parts, pieces, shares),
            out_shape=jax.ShapeDtypeStruct((own, sep), f32),
            in_specs=[
                pl.BlockSpec(memory_space=pltpu.HBM),
                pl.BlockSpec(memory_space=pltpu.HBM),
                pl.BlockSpec(memory_space=pltpu.SMEM),
                pl.BlockSpec(memory_space=pltpu.HBM),
                pl.BlockSpec(memory_space=pltpu.HBM),
            ],
            out_specs=pl.BlockSpec(memory_space=pltpu.VMEM),
            scratch_shapes=[
                pltpu.VMEM((sep, depth), jnp.bfloat16),
                pltpu.VMEM((sep, depth), jnp.bfloat16),
                pltpu.VMEM((count, blocks, rows, LANES), f32),
                pltpu.VMEM((count, blocks, rows, LANES), f32),
                pltpu.VMEM((2, count, pieces, rows, LANES), f32),
                dma((2, count)),
                dma((2, count, 3)),
                dma((count, steps)),
                dma((count, steps)),
                *[room(k) for k in range(steps + 1)],
                *[room(k + 1) for k in range(steps)],
                pltpu.VMEM((depth, sep), panels.dtype),
                pltpu.VMEM(eigvals.shape, f32),
                pltpu.VMEM(separator_diag.shape, f32),
                pltpu.VMEM(tables.shape, tables.dtype),
                dma((4,)),
            ],
            compiler_params=pltpu.CompilerParams(
                collective_id=0, has_side_effects=True, vmem_limit_bytes=48 * 2**20
            ),
        )(panels[0], eigvals, counts, separator_diag, tables)
        return root * (1.0 / math.sqrt(subs))

    return jax.shard_map(
        local,
        mesh=mesh,
        in_specs=(P("sub", "mode", None), P("sub", "mode"), P("sub"), P("sub", None), P()),
        out_specs=P("sub", None),
        check_vma=False,
    )
```

```python
import functools
import math

import jax
import jax.numpy as jnp
from jax import lax
from jax.experimental import pallas as pl
from jax.experimental.pallas import tpu as pltpu
from jax.sharding import PartitionSpec as P

MESH = pl.DeviceIdType.MESH
NT = (((1,), (1,)), ((), ()))
LANES = 128


def plan(subs, modes):
    if subs == 8 and modes == 4:
        x, y, near, far = ("mode", 1), ("sub", 0), ("sub", 1), ("sub", 2)
        return [
            [(True, *x), (True, *y), (True, *near), (True, *far)],
            [(True, *y), (True, *near), (True, *far), (False, *x)],
            [(True, *near), (True, *x), (True, *y), (True, *far)],
        ], 2, 2
    sub_bits, mode_bits = subs.bit_length() - 1, modes.bit_length() - 1
    steps = [(True, "sub", b) for b in range(sub_bits)]
    steps += [(False, "mode", b) for b in range(1, mode_bits)]
    return [steps] * 3, 1, 1


def bit_of(value, bit):
    return (value // 2**bit) % 2


def body(subs, modes, column_parts, pieces, shares, *refs):
    panels_hbm, eig_hbm, counts_ref, diag_hbm, tables_hbm, out_ref = refs[:6]
    panels_ref, eig_ref, diag_ref, tables_ref, load_sems = refs[-5:]
    wt, pt, to_core, from_core, fin, core_sems, fin_sems, send_sems, recv_sems = refs[6:15]
    parts = [part for part in column_parts for _ in range(shares)]
    order = [q * shares + h for h in range(shares) for q in range(len(column_parts))]
    steps = len(parts[0])
    accs = refs[15 : 15 + steps + 1]
    lands = refs[15 + steps + 1 : -5]
    count, chunks = len(parts), len(column_parts)
    loads = [
        pltpu.make_async_copy(source, kept, load_sems.at[i])
        for i, (source, kept) in enumerate(
            [
                (tables_hbm, tables_ref),
                (panels_hbm, panels_ref),
                (eig_hbm, eig_ref),
                (diag_hbm, diag_ref),
            ]
        )
    ]
    for load in loads:
        load.start()
    sub_me, mode_me = lax.axis_index("sub"), lax.axis_index("mode")
    core_me = mode_me % 2
    sep = panels_ref.shape[1]
    depth = panels_ref.shape[0]
    rows = sep // subs // pieces // shares
    place = {"sub": sub_me, "mode": mode_me}

    def partner(axis, bit):
        here = place[axis]
        other = here + 2**bit * (1 - 2 * bit_of(here, bit))
        return (other, mode_me) if axis == "sub" else (sub_me, other)

    sibling = partner("mode", 0)
    links = sorted({step[1:] for part in parts for step in part} | {("mode", 0)})
    barrier = pltpu.get_barrier_semaphore()
    for axis, bit in links:
        pl.semaphore_signal(barrier, inc=1, device_id=partner(axis, bit), device_id_type=MESH)

    first = lax.broadcasted_iota(jnp.int32, (sep, 1), 0)
    across = (sub_me, partner("mode", 1)[1] + 1 - 2 * core_me) if pieces == 2 else None
    greeted = len(links) + (pieces == 2)
    if pieces == 2:
        pl.semaphore_signal(barrier, inc=1, device_id=across, device_id_type=MESH)

    runs = sep // LANES
    place_in_run = lax.broadcasted_iota(jnp.int32, (LANES, sep), 0)
    run_row = lax.broadcasted_iota(jnp.int32, (8, sep), 0)
    run_of = lax.broadcasted_iota(jnp.int32, (8, LANES), 0)
    loads[0].wait()
    index = lax.broadcasted_iota(jnp.int32, (1, sep), 1)
    for level in reversed(range(subs.bit_length() - 1)):
        index = index + 97 * level % sep
        index = jnp.where(index >= sep, index - sep, index)
        line = (sub_me // 2**level) * 2**level + 2**level - 1
        row = tables_ref[pl.ds(line, 1), :]
        table = jnp.zeros((8, LANES), jnp.int32)
        for run in range(runs):
            table = jnp.where(run_of == run, row[:, run * LANES : (run + 1) * LANES], table)
        digits = jnp.concatenate([table // 16, table % 16], axis=0).astype(jnp.float32).astype(jnp.bfloat16)
        mark = jnp.where(place_in_run == index % LANES, 1.0, 0.0).astype(jnp.bfloat16)
        found = jnp.dot(digits, mark, preferred_element_type=jnp.float32)
        value = jnp.where(run_row == index // LANES, found[0:8] * 16.0 + found[8:16], 0.0)
        index = jnp.sum(value, axis=0, keepdims=True).astype(jnp.int32)
    target = jnp.broadcast_to(index, (8, sep)).T[:, 0:1]
    lanes = lax.broadcasted_iota(jnp.int32, (sep, sep), 1)
    moved = jnp.where(target == lanes, 1.0, 0.0).astype(jnp.bfloat16)

    for load in loads[1:]:
        load.wait()
    live = lax.broadcasted_iota(jnp.int32, (1, depth), 1) + mode_me * depth < counts_ref[0]
    minus_scale = jnp.where(live, -1.0, 0.0) / eig_ref[...]
    panels_t = lax.dot_general(moved, panels_ref[...], NT, preferred_element_type=jnp.float32)
    pt[...] = panels_t.astype(jnp.bfloat16)
    wt[...] = (panels_t * minus_scale).astype(jnp.bfloat16)

    columns = lax.broadcasted_iota(jnp.int32, (sep, LANES), 1)

    def tile(core, p):
        start = pl.multiple_of((core * chunks + p) * LANES, LANES)
        return lax.dot_general(
            wt[...], pt[pl.ds(start, LANES), :], NT, preferred_element_type=jnp.float32
        )

    def on_diag(core, p):
        return columns + (core * chunks + p) * LANES == first

    def slot_of(p, block):
        slot, taken = 0, 0
        for halve, axis, bit in parts[p]:
            if halve:
                if axis == "sub":
                    far = (bit_of(block // pieces, bit) + bit_of(sub_me, bit)) % 2
                else:
                    far = (bit_of(block % pieces, bit - 1) + bit_of(mode_me, bit)) % 2
                    taken = 1
                slot = slot * 2 + far
        return slot if taken else slot * pieces + block % pieces

    def core_copy(p):
        return pltpu.make_async_remote_copy(
            to_core.at[p], from_core.at[p], core_sems.at[0, p], core_sems.at[1, p], sibling, MESH
        )

    blocks = subs * pieces
    def store_tile(kept, chunk, value):
        for b in range(blocks):
            slot = slot_of(chunk * shares, b)
            for h in range(shares):
                at = (b * shares + h) * rows
                kept[chunk * shares + h, slot, :, :] = value[at : at + rows]

    for chunk in range(chunks):
        store_tile(to_core, chunk, tile(1 - core_me, chunk))
        if chunk == 0:
            pl.semaphore_wait(barrier, greeted)
        for h in range(shares):
            core_copy(chunk * shares + h).start()

    sizes = []
    for p in range(count):
        n, own = blocks, []
        for halve, _, _ in parts[p]:
            n = n // 2 if halve else n
            own.append(n)
        sizes.append(own)

    def exchange(p, k):
        halve, axis, bit = parts[p][k]
        n = sizes[p][k]
        return pltpu.make_async_remote_copy(
            accs[k].at[p, pl.ds(n if halve else 0, n)],
            lands[k].at[p, pl.ds(0, n)],
            send_sems.at[p, k],
            recv_sems.at[p, k],
            partner(axis, bit),
            MESH,
        )

    diag = diag_ref[...] * jnp.where(mode_me // 2 == 0, 1.0, 0.0)
    top = diag.astype(jnp.bfloat16).astype(jnp.float32)
    middle = (diag - top).astype(jnp.bfloat16).astype(jnp.float32)
    low = diag - top - middle
    pick = lax.broadcasted_iota(jnp.int32, (16, sep), 0)
    split = jnp.where(pick == 0, top, jnp.where(pick == 1, middle, jnp.where(pick == 2, low, 0.0)))
    got = lax.dot_general(moved, split.astype(jnp.bfloat16), NT, preferred_element_type=jnp.float32)
    diag_moved = got[:, 0:1] + got[:, 1:2] + got[:, 2:3]
    for chunk in range(chunks):
        placed = jnp.where(on_diag(core_me, chunk), diag_moved, 0.0)
        store_tile(accs[0], chunk, tile(core_me, chunk) + placed)
    for p in order:
        core_copy(p).wait_recv()
        accs[0][p] = accs[0][p] + from_core[p]
        exchange(p, 0).start()

    cut = [any(halve and axis == "mode" for halve, axis, _ in part) for part in parts]
    piece_me = bit_of(mode_me, 1)

    def last_copies(p):
        spot = fin.at[core_me, p, pl.ds(piece_me, 1)] if cut[p] else fin.at[core_me, p]
        targets = [sibling, partner("mode", 1), across] if cut[p] else [sibling]
        return [
            pltpu.make_async_remote_copy(spot, spot, fin_sems.at[0, p, i], fin_sems.at[1, p, i], target, MESH)
            for i, target in enumerate(targets)
        ]

    for k in range(steps):
        for p in order:
            n = sizes[p][k]
            exchange(p, k).wait_recv()
            total = accs[k][p, 0:n] + lands[k][p, 0:n]
            if k < steps - 1:
                accs[k + 1][p, 0:n] = total
                exchange(p, k + 1).start()
                continue
            if cut[p]:
                fin[core_me, p, pl.ds(piece_me, 1)] = total
            else:
                fin[core_me, p] = total
            for copy in last_copies(p):
                copy.start()
    for p in order:
        for copy in last_copies(p):
            copy.wait_recv()
    for c in range(2):
        for p in range(count):
            at = (c * chunks + p // shares) * LANES
            for piece in range(pieces):
                down = (piece * shares + p % shares) * rows
                out_ref[down : down + rows, at : at + LANES] = fin[c, p, piece]
    for p in range(count):
        core_copy(p).wait_send()
        for k in range(steps):
            exchange(p, k).wait_send()
        for copy in last_copies(p):
            copy.wait_send()


def solution(mesh):
    subs, modes = mesh.shape["sub"], mesh.shape["mode"]
    column_parts, pieces, shares = plan(subs, modes)
    parts = [part for part in column_parts for _ in range(shares)]

    def local(panels, eigvals, counts, separator_diag, tables):
        sep, depth = panels.shape[2], panels.shape[1]
        own = sep // subs
        rows = own // pieces // shares
        count, steps, blocks = len(parts), len(parts[0]), subs * pieces
        f32 = jnp.float32

        def room(k):
            most = 0
            for part in parts:
                n = blocks
                for halve, _, _ in part[:k]:
                    n = n // 2 if halve else n
                most = max(most, n)
            return pltpu.VMEM((count, most, rows, LANES), f32)

        dma = pltpu.SemaphoreType.DMA
        root = pl.pallas_call(
            functools.partial(body, subs, modes, column_parts, pieces, shares),
            out_shape=jax.ShapeDtypeStruct((own, sep), f32),
            in_specs=[
                pl.BlockSpec(memory_space=pltpu.HBM),
                pl.BlockSpec(memory_space=pltpu.HBM),
                pl.BlockSpec(memory_space=pltpu.SMEM),
                pl.BlockSpec(memory_space=pltpu.HBM),
                pl.BlockSpec(memory_space=pltpu.HBM),
            ],
            out_specs=pl.BlockSpec(memory_space=pltpu.VMEM),
            scratch_shapes=[
                pltpu.VMEM((sep, depth), jnp.bfloat16),
                pltpu.VMEM((sep, depth), jnp.bfloat16),
                pltpu.VMEM((count, blocks, rows, LANES), f32),
                pltpu.VMEM((count, blocks, rows, LANES), f32),
                pltpu.VMEM((2, count, pieces, rows, LANES), f32),
                dma((2, count)),
                dma((2, count, 3)),
                dma((count, steps)),
                dma((count, steps)),
                *[room(k) for k in range(steps + 1)],
                *[room(k + 1) for k in range(steps)],
                pltpu.VMEM((depth, sep), panels.dtype),
                pltpu.VMEM(eigvals.shape, f32),
                pltpu.VMEM(separator_diag.shape, f32),
                pltpu.VMEM(tables.shape, tables.dtype),
                dma((4,)),
            ],
            compiler_params=pltpu.CompilerParams(
                collective_id=0, has_side_effects=True, vmem_limit_bytes=48 * 2**20
            ),
        )(panels[0], eigvals, counts, separator_diag, tables)
        return root * (1.0 / math.sqrt(subs))

    return jax.shard_map(
        local,
        mesh=mesh,
        in_specs=(P("sub", "mode", None), P("sub", "mode"), P("sub"), P("sub", None), P()),
        out_specs=P("sub", None),
        check_vma=False,
    )
```
